512 devices in a mesh: depth: 64 (over x_hi, z, core), lat: 8 (over y, x_lo).
Axes of the slice: x: 4 (x_hi: 2, x_lo: 2; x = x_hi * 2 + x_lo), y: 4, z: 16, core: 2. Of those that a mesh axis runs over, the one named last changes fastest.
Arguments:
- in_flight: float32 [64, 4, 256, 256], P('depth', None, 'lat'), may hold values from -6 to 6
- entering: float32 [2, 4, 256, 256], P(None, None, 'lat'), may hold values from -6 to 6
- classes: int32 [64, 256, 256], P('depth', 'lat'), may hold values from 0 to 31
- freq_phase: float32 [66], replicated, may hold values from 4 to 8.5
- class_slowness: float32 [32], replicated, may hold values from 0.8 to 1.4
Outputs:
- images: float32 [64, 8, 256, 256], P('depth', None, 'lat')
- wave_out: float32 [64, 4, 256, 256], P('depth', None, 'lat')
The draws below stay inside these ranges and needn't reach their ends.
All inputs are finite; a program needn't handle non-finite values.
Results may differ from the reference program's by a relative error of at most 0.0003.
Values sent between devices are 32-bit elements; how exact they have to be, the bound alone decides.
A program may use at most 64 MiB of HBM per device.

```python
import math
import jax
import jax.numpy as jnp
from jax import lax

NX = 256
TERMS = 16
OFFSETS = 8
CLASSES = 32
TURNS = 3
NZ = 64
NY = 256
FREQS = 66


def plant(values, key, smallest, top_value):
    longest = values.shape.index(max(values.shape))
    spots = []
    for shift in (0, 1):
        where = [jax.random.randint(jax.random.fold_in(key, axis), (), 0, length) for axis, length in enumerate(values.shape)]
        where[longest] = (where[longest] + shift) % values.shape[longest]
        spots.append(tuple(where))
    return values.at[spots[0]].set(smallest).at[spots[1]].set(top_value)


def steps_of(stream_key, dims, shards, smallest, high):
    def one(position, blocks):
        draws = jax.random.uniform(jax.random.fold_in(jax.random.fold_in(stream_key, 6), position), (blocks,), jnp.float32, smallest / len(shards), high / len(shards))
        return jnp.repeat(jnp.exp(draws), dims[position] // blocks).reshape((-1,) + (1,) * (len(dims) - position - 1))

    loudness = one(*shards[0])
    for cut in shards[1:]:
        loudness = loudness * one(*cut)
    return loudness


def noise(own_key, extent, spread, bound, shards=(), kind=jnp.bfloat16):
    loudness = steps_of(own_key, extent, shards, -0.22, 0.18) if shards else 1.0
    values = jax.random.normal(own_key, extent, jnp.float32) * spread * loudness
    return jnp.minimum(jnp.maximum(values, -bound), bound).astype(kind)


def setup_inputs(seed: int = 0) -> dict:
    key_of = jax.random.split(jax.random.key(seed), 6)
    in_flight = noise(key_of[0], (NZ, 4, NY, NX), 1.0, 6.0, ((0, 64), (2, 8)), jnp.float32)
    entering = noise(key_of[1], (TURNS - 1, 4, NY, NX), 1.0, 6.0, ((2, 8),), jnp.float32)
    classes = plant(jax.random.randint(key_of[2], (NZ, NY, NX), 0, CLASSES), jax.random.fold_in(key_of[2], 1), 0, CLASSES - 1).astype(jnp.int32)
    freq_phase = jnp.clip(jnp.exp(jax.random.uniform(key_of[3], (FREQS,), jnp.float32, math.log(4.0), math.log(8.5))), 4.0, 8.5)
    class_slowness = jnp.clip(jnp.exp(jax.random.uniform(key_of[4], (CLASSES,), jnp.float32, math.log(0.8), math.log(1.4))), 0.8, 1.4)
    return dict(in_flight=in_flight, entering=entering, classes=classes, freq_phase=freq_phase, class_slowness=class_slowness)


hale_weight = 0.0255
centre_weight = -0.5 + hale_weight
edge_weight = 0.25 - 0.5 * hale_weight
corner_weight = 0.125 + 0.25 * hale_weight
miller_start = 32


def stencil(padded):
    centre = padded[:, 1:-1, 1:-1]
    edge_sum = padded[:, :-2, 1:-1] + padded[:, 2:, 1:-1] + padded[:, 1:-1, :-2] + padded[:, 1:-1, 2:]
    corners = padded[:, :-2, :-2] + padded[:, :-2, 2:] + padded[:, 2:, :-2] + padded[:, 2:, 2:]
    return centre_weight * centre + edge_weight * edge_sum + corner_weight * corners


def bessel_table(phases):
    values = [None] * (miller_start + 1)
    upper = jnp.zeros_like(phases)
    current = jnp.ones_like(phases)
    values[miller_start] = current
    for k in range(miller_start, 0, -1):
        lower = (2.0 * k / phases) * current - upper
        values[k - 1] = lower
        upper, current = current, lower
    evens = values[2]
    for k in range(4, miller_start + 1, 2):
        evens = evens + values[k]
    scale = values[0] + 2.0 * evens
    result = []
    for k in range(TERMS):
        ratio = values[k] / scale
        result.append(ratio if k == 0 else 2.0 * ratio)
    return jnp.stack(result)


def rotate(coefficient, k, fields):
    cycle_real = jnp.array([1.0, 0.0, -1.0, 0.0], fields.dtype)
    cycle_imag = jnp.array([0.0, 1.0, 0.0, -1.0], fields.dtype)
    real_part = coefficient * cycle_real[k % 4]
    imag_part = coefficient * cycle_imag[k % 4]
    return jnp.stack([real_part * fields[0] - imag_part * fields[1],
                      real_part * fields[1] + imag_part * fields[0],
                      real_part * fields[2] + imag_part * fields[3],
                      real_part * fields[3] - imag_part * fields[2]])


def correlate(extended, strip_rows):
    half_offset = OFFSETS // 2
    products = []
    for o in range(OFFSETS):
        lag = o - half_offset
        source = extended[:, half_offset - lag:half_offset - lag + strip_rows]
        receiver = extended[:, half_offset + lag:half_offset + lag + strip_rows]
        products.append(source[0] * receiver[2] + source[1] * receiver[3])
    return jnp.stack(products)


def extrapolate(fields, bessel):
    def apply_whole(current):
        return stencil(jnp.pad(current, ((0, 0), (1, 1), (1, 1))))

    first_term = apply_whole(fields)
    summed = rotate(bessel[0], 0, fields) + rotate(bessel[1], 1, first_term)

    def advance(k, carried):
        previous, current, running = carried
        following = 2.0 * apply_whole(current) - previous
        coefficient = lax.dynamic_index_in_dim(bessel, k + 1, 0, False)
        return (current, following, running + rotate(coefficient, k + 1, following))

    return lax.fori_loop(1, TERMS - 1, advance, (fields, first_term, summed))[2]


def reference(in_flight, entering, classes, freq_phase, class_slowness):
    wavefield = in_flight
    images = jnp.zeros((NZ, OFFSETS, NY, NX), in_flight.dtype)
    slab_ids = jnp.arange(NZ, dtype=jnp.int32)
    half_offset = OFFSETS // 2
    advanced = in_flight
    for turn_index in range(TURNS):
        freq_ids = (turn_index + NZ - 1 - slab_ids).astype(jnp.int32)

        def per_slab(inputs):
            fields, slab_classes, freq_index = inputs
            coeff_table = bessel_table(freq_phase[freq_index] * class_slowness)
            bessel = coeff_table[:, slab_classes]
            moved_on = extrapolate(fields, bessel)
            extended = jnp.pad(moved_on, ((0, 0), (half_offset, half_offset), (0, 0)))
            return moved_on, correlate(extended, NY)

        advanced, partial_value = lax.map(per_slab, (wavefield, classes, freq_ids))
        images = images + partial_value
        if turn_index + 1 < TURNS:
            wavefield = jnp.concatenate([entering[turn_index][None], advanced[:-1]], 0)
    return images, advanced
```

```python
import jax
import jax.numpy as jnp
from jax import lax
from jax.experimental import pallas as pl
from jax.experimental.pallas import tpu as pltpu
from jax.sharding import PartitionSpec as P

TERMS = 16
OFFSETS = 8
TURNS = 3
STRIP = 32
HALO = 19
ROWS = STRIP + 2 * HALO
FOLD = ROWS // 2
REACH = 15
KEPT = FOLD - REACH
PLANE = 48
MESH = pl.DeviceIdType.MESH

hale_weight = 0.0255
centre_weight = -0.5 + hale_weight
edge_weight = 0.25 - 0.5 * hale_weight
corner_weight = 0.125 + 0.25 * hale_weight
kappa = edge_weight / corner_weight
delta = centre_weight - edge_weight * kappa
miller_start = 32


def lane_gather(x, idx):
    numbers = lax.GatherDimensionNumbers(
        offset_dims=(),
        collapsed_slice_dims=(1,),
        start_index_map=(1,),
        operand_batching_dims=(0,),
        start_indices_batching_dims=(0,),
    )
    return lax.gather(
        x, idx[:, :, None], numbers, (1, 1), mode=lax.GatherScatterMode.PROMISE_IN_BOUNDS
    )


def kernel(
    inflight_ref, entering_ref, classes_ref, freq_ref, slow_ref,
    images_ref, wave_ref,
    raw, raw_cls, cls_up, cls_dn, pr, adv, ta, tb, acc_e, acc_o, coef, cls, table, std, img, wout,
    in_sem, out_sem, ssem, rsem, esem, cssem, crsem,
):
    d = lax.axis_index("depth")
    l = lax.axis_index("lat")
    D = lax.axis_size("depth")
    L = lax.axis_size("lat")

    sub = lax.broadcasted_iota(jnp.int32, (8, 128), 0)
    lane = lax.broadcasted_iota(jnp.int32, (8, 128), 1)
    low = sub < 4

    def roll4(x):
        return pltpu.roll(x, 4, 0)

    def load_fields(src, slot):
        return [
            pltpu.make_async_copy(
                src.at[f, :, pl.ds(h * 128, 128)],
                raw.at[slot, pl.ds((h * 4 + f) * STRIP, STRIP)],
                in_sem.at[slot, h * 4 + f],
            )
            for h in range(2)
            for f in range(4)
        ]

    for c in load_fields(inflight_ref.at[0], 0):
        c.start()
    cls_copy = pltpu.make_async_copy(classes_ref.at[0], raw_cls, in_sem.at[TURNS, 0])
    cls_copy.start()

    @pl.when(d == 0)
    def _():
        for t in range(TURNS - 1):
            for c in load_fields(entering_ref.at[t], t + 1):
                c.start()

    bar = pltpu.get_barrier_semaphore()
    has_up, has_dn, has_next, has_prev = l > 0, l < L - 1, d < D - 1, d > 0

    def greet(cond, dd, dl):
        @pl.when(cond)
        def _():
            pl.semaphore_signal(bar, inc=1, device_id=(d + dd, l + dl), device_id_type=MESH)

    greet(has_up, 0, -1)
    greet(has_dn, 0, 1)
    greet(has_prev, -1, 0)
    greet(jnp.logical_and(has_prev, has_up), -1, -1)
    greet(jnp.logical_and(has_prev, has_dn), -1, 1)

    zero = jnp.zeros((8, 128), jnp.float32)

    @pl.when(l == 0)
    def _():
        for t in range(TURNS):
            for i in range(HALO):
                pr[t, i] = zero
        cls_up[...] = jnp.zeros_like(cls_up)

    @pl.when(l == L - 1)
    def _():
        for t in range(TURNS):
            for i in range(HALO):
                pr[t, HALO + STRIP + i] = zero
        cls_dn[...] = jnp.zeros_like(cls_dn)

    keep = jnp.where(
        low, jnp.where(l > 0, 1.0, 0.0).astype(jnp.float32), jnp.where(l < L - 1, 1.0, 0.0).astype(jnp.float32)
    )

    pack_idx = 2 * jnp.bitwise_and(lane, 63) + jnp.where(low, 0, 1)
    pack_direct = (lane < 64) == low

    def pack_fields(slot):
        def body(y, _):
            v = raw[slot, pl.ds(y, 8, stride=STRIP), :]
            a = lane_gather(v, pack_idx)
            b = lane_gather(roll4(v), pack_idx)
            pr[slot, HALO + y] = jnp.where(pack_direct, a, b)
            return 0

        lax.fori_loop(0, STRIP, body, 0, unroll=8)

    for c in load_fields(inflight_ref.at[0], 0):
        c.wait()
    pack_fields(0)

    n_lat = has_up.astype(jnp.int32) + has_dn.astype(jnp.int32)
    pl.semaphore_wait(bar, n_lat + has_next.astype(jnp.int32) * (1 + n_lat))
    cls_copy.wait()

    def to_up(src, slot, dd, sem):
        return pltpu.make_async_remote_copy(
            src, pr.at[slot, pl.ds(HALO + STRIP, HALO)], sem, rsem.at[slot, 1],
            device_id=(d + dd, l - 1), device_id_type=MESH,
        )

    def to_dn(src, slot, dd, sem):
        return pltpu.make_async_remote_copy(
            src, pr.at[slot, pl.ds(0, HALO)], sem, rsem.at[slot, 2],
            device_id=(d + dd, l + 1), device_id_type=MESH,
        )

    def lat_sends(slot):
        up = to_up(pr.at[slot, pl.ds(HALO, HALO)], slot, 0, esem.at[slot, 0])
        dn = to_dn(pr.at[slot, pl.ds(STRIP, HALO)], slot, 0, esem.at[slot, 1])
        return up, dn

    def cls_sends():
        up = pltpu.make_async_remote_copy(
            raw_cls.at[pl.ds(0, 8)], cls_dn, cssem.at[0], crsem.at[0], device_id=(d, l - 1), device_id_type=MESH
        )
        dn = pltpu.make_async_remote_copy(
            raw_cls.at[pl.ds(STRIP - 8, 8)], cls_up, cssem.at[1], crsem.at[1], device_id=(d, l + 1), device_id_type=MESH
        )
        return up, dn

    @pl.when(has_up)
    def _():
        lat_sends(0)[0].start()
        cls_sends()[0].start()

    @pl.when(has_dn)
    def _():
        lat_sends(0)[1].start()
        cls_sends()[1].start()

    @pl.when(d == 0)
    def _():
        for t in range(1, TURNS):
            for c in load_fields(entering_ref.at[t - 1], t):
                c.wait()
            pack_fields(t)

    @pl.when(jnp.logical_and(d == 0, has_up))
    def _():
        for t in range(1, TURNS):
            lat_sends(t)[0].start()

    @pl.when(jnp.logical_and(d == 0, has_dn))
    def _():
        for t in range(1, TURNS):
            lat_sends(t)[1].start()

    cid = jnp.bitwise_and(lane, 31)
    slow = jnp.zeros((8, 128), jnp.float32)
    for c in range(32):
        slow = jnp.where(cid == c, slow_ref[c], slow)
    for t in range(TURNS):
        inv = 1.0 / (freq_ref[t + D - 1 - d] * slow)
        values = [None] * (miller_start + 1)
        upper = jnp.zeros_like(inv)
        current = jnp.ones_like(inv)
        values[miller_start] = current
        for k in range(miller_start, 0, -1):
            lower = (2.0 * k * inv) * current - upper
            values[k - 1] = lower
            upper, current = current, lower
        evens = values[2]
        for k in range(4, miller_start + 1, 2):
            evens = evens + values[k]
        scale = 1.0 / (values[0] + 2.0 * evens)
        for k in range(TERMS):
            sign = -1.0 if (k // 2) % 2 else 1.0
            table[t, k] = values[k] * scale * (sign if k == 0 else 2.0 * sign)

    half_lane = lane < 64
    even_idx = 2 * jnp.bitwise_and(lane, 63)

    def fold_classes(i, top, top_row, bottom, bottom_row):
        sides = []
        for h in range(2):
            a = jnp.broadcast_to(top[pl.ds(top_row, 1), h * 128 : (h + 1) * 128], (8, 128))
            b = jnp.broadcast_to(bottom[pl.ds(bottom_row, 1), h * 128 : (h + 1) * 128], (8, 128))
            sides.append(jnp.where(low, a, b))
        for p in range(2):
            cls[i, p] = jnp.where(
                half_lane, lane_gather(sides[0], even_idx + p), lane_gather(sides[1], even_idx + p)
            )

    @pl.when(has_up)
    def _():
        cls_sends()[1].wait_recv()

    @pl.when(has_dn)
    def _():
        cls_sends()[0].wait_recv()

    for i in range(4):
        fold_classes(i, cls_up, 4 + i, cls_dn, 3 - i)
    for i in range(4, KEPT):
        fold_classes(i, raw_cls, i - 4, raw_cls, STRIP + 3 - i)

    def look_up(t):
        def body(i, _):
            for p in range(2):
                c = cls[i, p]
                for k in range(TERMS):
                    coef[k, i, p] = lane_gather(table[t, k], c)
            return 0

        lax.fori_loop(0, KEPT, body, 0)

    def step(cur, prev, low_row, k, first, even):
        acc = acc_e if even else acc_o
        c1 = corner_weight * (1.0 if first else 2.0)
        c2 = delta * (1.0 if first else 2.0)
        above = [cur[low_row - 1, p] for p in range(2)]
        here = [cur[low_row, p] for p in range(2)]
        for i in range(low_row, FOLD):
            if i < FOLD - 1:
                below = [cur[i + 1, p] for p in range(2)]
            else:
                below = [roll4(v) for v in here]
            w = [(above[p] + below[p]) + kappa * here[p] for p in range(2)]
            from_odd = jnp.where(lane == 0, 0.0, pltpu.roll(w[1], 1, 1))
            from_even = jnp.where(lane == 127, 0.0, pltpu.roll(w[0], 127, 1))
            x = [from_odd + w[1], w[0] + from_even]
            for p in range(2):
                f = c1 * (x[p] + kappa * w[p]) + c2 * here[p]
                if not first:
                    f = f - prev[i, p]
                if i < HALO:
                    f = f * keep
                prev[i, p] = f
                if i >= REACH:
                    j = i - REACH
                    if first:
                        acc[j, p] = coef[k, j, p] * f
                    else:
                        acc[j, p] = acc[j, p] + coef[k, j, p] * f
            above, here = here, below

    swap_sign = jnp.where(jnp.logical_or(jnp.bitwise_and(sub, 3) == 0, jnp.bitwise_and(sub, 3) == 3), -1.0, 1.0).astype(jnp.float32)
    even_sub = jnp.bitwise_and(sub, 1) == 0

    def extrapolate(t):
        def unfold(i):
            a = pr[t, i]
            b = pr[t, ROWS - 1 - i]
            return jnp.where(low, a, roll4(b)), jnp.where(low, roll4(a), b)

        def body0(i, _):
            e, o = unfold(i)
            ta[i, 0] = e
            ta[i, 1] = o
            return 0

        def body1(i, _):
            e, o = unfold(i)
            ta[i, 0] = e
            ta[i, 1] = o
            acc_e[i - REACH, 0] = coef[0, i - REACH, 0] * e
            acc_e[i - REACH, 1] = coef[0, i - REACH, 1] * o
            return 0

        lax.fori_loop(0, REACH, body0, 0, unroll=5)
        lax.fori_loop(REACH, FOLD, body1, 0, unroll=5)

        step(ta, tb, 1, 1, True, False)

        def pair(base):
            def body(n, _):
                k = base + 2 * n
                step(tb, ta, base, k, False, True)
                step(ta, tb, base + 1, k + 1, False, False)
                return 0

            return body

        lax.fori_loop(0, 2, pair(2), 0)
        lax.fori_loop(0, 2, pair(6), 0)
        lax.fori_loop(0, 2, pair(10), 0)
        lax.fori_loop(0, 1, pair(14), 0)

        def join(i, _):
            out = []
            for p in range(2):
                o = acc_o[i, p]
                swapped = jnp.where(even_sub, pltpu.roll(o, 7, 0), pltpu.roll(o, 1, 0))
                out.append(acc_e[i, p] + swap_sign * swapped)
            adv[t, i] = jnp.where(low, out[0], roll4(out[1]))
            adv[t, 2 * KEPT - 1 - i] = jnp.where(low, roll4(out[0]), out[1])
            return 0

        lax.fori_loop(0, KEPT, join, 0, unroll=5)

    def correlate(t):
        def spread(r, _):
            std[pl.ds(r, 8, stride=PLANE), :] = adv[t, r]
            return 0

        lax.fori_loop(0, 2 * KEPT, spread, 0, unroll=8)
        for p in range(2):
            for b in range(STRIP // 8):
                for o in range(OFFSETS):
                    g = o - OFFSETS // 2
                    s0 = std[pl.ds((p * 4 + 0) * PLANE + 4 - g + 8 * b, 8), :]
                    s1 = std[pl.ds((p * 4 + 1) * PLANE + 4 - g + 8 * b, 8), :]
                    r0 = std[pl.ds((p * 4 + 2) * PLANE + 4 + g + 8 * b, 8), :]
                    r1 = std[pl.ds((p * 4 + 3) * PLANE + 4 + g + 8 * b, 8), :]
                    value = s0 * r0 + s1 * r1
                    if t > 0:
                        value = value + img[p, o, b]
                    img[p, o, b] = value

    def hand_over(t):
        n = t + 1
        strip = pltpu.make_async_remote_copy(
            adv.at[t, pl.ds(4, STRIP)], pr.at[n, pl.ds(HALO, STRIP)], ssem.at[t, 0], rsem.at[n, 0],
            device_id=(d + 1, l), device_id_type=MESH,
        )
        up = to_up(adv.at[t, pl.ds(4, HALO)], n, 1, ssem.at[t, 1])
        dn = to_dn(adv.at[t, pl.ds(4 + STRIP - HALO, HALO)], n, 1, ssem.at[t, 2])
        return strip, up, dn

    next_up = jnp.logical_and(has_next, has_up)
    next_dn = jnp.logical_and(has_next, has_dn)

    def for_each_send(t, act):
        for cond, which in ((next_up, 1), (next_dn, 2), (has_next, 0)):
            @pl.when(cond)
            def _():
                act(hand_over(t)[which])

    def wait_halo(t):
        @pl.when(has_dn)
        def _():
            lat_sends(t)[0].wait_recv()

        @pl.when(has_up)
        def _():
            lat_sends(t)[1].wait_recv()

    look_up(0)
    for t in range(TURNS):
        wait_halo(t)
        if t > 0:
            @pl.when(has_prev)
            def _():
                hand_over(t - 1)[0].wait_recv()
        extrapolate(t)
        if t + 1 < TURNS:
            for_each_send(t, lambda c: c.start())
            correlate(t)
            look_up(t + 1)

    join_idx = lax.shift_right_logical(lane, 1) + jnp.where(low, 0, 64)
    join_direct = (jnp.bitwise_and(lane, 1) == 0) == low

    def put(y, _):
        v = adv[TURNS - 1, 4 + y]
        a = lane_gather(v, join_idx)
        b = lane_gather(roll4(v), join_idx)
        wout[pl.ds(y, 8, stride=STRIP), :] = jnp.where(join_direct, a, b)
        return 0

    lax.fori_loop(0, STRIP, put, 0, unroll=8)

    def stores():
        return [
            pltpu.make_async_copy(
                wout.at[pl.ds((h * 4 + f) * STRIP, STRIP)],
                wave_ref.at[0, f, :, pl.ds(h * 128, 128)],
                out_sem.at[h * 4 + f],
            )
            for h in range(2)
            for f in range(4)
        ]

    for c in stores():
        c.start()
    correlate(TURNS - 1)
    half_idx = lax.shift_right_logical(lane, 1)
    even_lane = jnp.bitwise_and(lane, 1) == 0
    for o in range(OFFSETS):
        for b in range(STRIP // 8):
            e, q = img[0, o, b], img[1, o, b]
            for h in range(2):
                images_ref[0, o, pl.ds(8 * b, 8), pl.ds(128 * h, 128)] = jnp.where(
                    even_lane, lane_gather(e, half_idx + 64 * h), lane_gather(q, half_idx + 64 * h)
                )

    @pl.when(has_up)
    def _():
        lat_sends(0)[0].wait_send()
        cls_sends()[0].wait_send()

    @pl.when(has_dn)
    def _():
        lat_sends(0)[1].wait_send()
        cls_sends()[1].wait_send()

    @pl.when(jnp.logical_and(d == 0, has_up))
    def _():
        for t in range(1, TURNS):
            lat_sends(t)[0].wait_send()

    @pl.when(jnp.logical_and(d == 0, has_dn))
    def _():
        for t in range(1, TURNS):
            lat_sends(t)[1].wait_send()

    for t in range(TURNS - 1):
        for_each_send(t, lambda c: c.wait_send())
    for c in stores():
        c.wait()


def local(in_flight, entering, classes, freq_phase, class_slowness):
    any_space = pl.BlockSpec(memory_space=pl.ANY)
    smem = pl.BlockSpec(memory_space=pltpu.SMEM)
    f32, i32 = jnp.float32, jnp.int32
    dma = pltpu.SemaphoreType.DMA
    return pl.pallas_call(
        kernel,
        out_shape=(
            jax.ShapeDtypeStruct((1, OFFSETS, STRIP, 256), f32),
            jax.ShapeDtypeStruct((1, 4, STRIP, 256), f32),
        ),
        in_specs=[any_space, any_space, any_space, smem, smem],
        out_specs=(pl.BlockSpec(memory_space=pltpu.VMEM), any_space),
        scratch_shapes=[
            pltpu.VMEM((TURNS, 8 * STRIP, 128), f32),
            pltpu.VMEM((STRIP, 256), i32),
            pltpu.VMEM((8, 256), i32),
            pltpu.VMEM((8, 256), i32),
            pltpu.VMEM((TURNS, ROWS, 8, 128), f32),
            pltpu.VMEM((TURNS, 2 * KEPT, 8, 128), f32),
            pltpu.VMEM((FOLD, 2, 8, 128), f32),
            pltpu.VMEM((FOLD, 2, 8, 128), f32),
            pltpu.VMEM((KEPT, 2, 8, 128), f32),
            pltpu.VMEM((KEPT, 2, 8, 128), f32),
            pltpu.VMEM((TERMS, KEPT, 2, 8, 128), f32),
            pltpu.VMEM((KEPT, 2, 8, 128), i32),
            pltpu.VMEM((TURNS, TERMS, 8, 128), f32),
            pltpu.VMEM((8 * PLANE, 128), f32),
            pltpu.VMEM((2, OFFSETS, STRIP // 8, 8, 128), f32),
            pltpu.VMEM((8 * STRIP, 128), f32),
            dma((TURNS + 1, 8)),
            dma((8,)),
            dma((TURNS - 1, 3)),
            dma((TURNS, 3)),
            dma((TURNS, 2)),
            dma((2,)),
            dma((2,)),
        ],
        compiler_params=pltpu.CompilerParams(
            collective_id=0, has_side_effects=True, vmem_limit_bytes=40 * 2**20
        ),
        cost_estimate=pl.CostEstimate(flops=60_000_000, bytes_accessed=1_000_000, transcendentals=0),
    )(in_flight, entering, classes, freq_phase, class_slowness)


def solution(mesh):
    in_specs = (
        P("depth", None, "lat", None),
        P(None, None, "lat", None),
        P("depth", "lat", None),
        P(),
        P(),
    )
    out_specs = (P("depth", None, "lat", None), P("depth", None, "lat", None))
    return jax.shard_map(local, mesh=mesh, in_specs=in_specs, out_specs=out_specs, check_vma=False)
```

```python
import jax
import jax.numpy as jnp
from jax import lax
from jax.experimental import pallas as pl
from jax.experimental.pallas import tpu as pltpu
from jax.sharding import PartitionSpec as P

TERMS = 16
OFFSETS = 8
TURNS = 3
STRIP = 32
HALO = 19
ROWS = STRIP + 2 * HALO
FOLD = ROWS // 2
REACH = 15
KEPT = FOLD - REACH
PLANE = 48
MESH = pl.DeviceIdType.MESH

hale_weight = 0.0255
centre_weight = -0.5 + hale_weight
edge_weight = 0.25 - 0.5 * hale_weight
corner_weight = 0.125 + 0.25 * hale_weight
kappa = edge_weight / corner_weight
delta = centre_weight - edge_weight * kappa
miller_start = 32


def lane_gather(x, idx):
    numbers = lax.GatherDimensionNumbers(
        offset_dims=(),
        collapsed_slice_dims=(1,),
        start_index_map=(1,),
        operand_batching_dims=(0,),
        start_indices_batching_dims=(0,),
    )
    return lax.gather(
        x, idx[:, :, None], numbers, (1, 1), mode=lax.GatherScatterMode.PROMISE_IN_BOUNDS
    )


def kernel(
    inflight_ref, entering_ref, classes_ref, freq_ref, slow_ref,
    images_ref, wave_ref,
    raw, raw_cls, cls_up, cls_dn, pr, adv, ta, tb, acc_e, acc_o, coef, cls, table, std, img, wout,
    in_sem, out_sem, ssem, rsem, esem, cssem, crsem,
):
    d = lax.axis_index("depth")
    l = lax.axis_index("lat")
    D = lax.axis_size("depth")
    L = lax.axis_size("lat")

    sub = lax.broadcasted_iota(jnp.int32, (8, 128), 0)
    lane = lax.broadcasted_iota(jnp.int32, (8, 128), 1)
    low = sub < 4

    def roll4(x):
        return pltpu.roll(x, 4, 0)

    def load_fields(src, slot):
        return [
            pltpu.make_async_copy(
                src.at[f, :, pl.ds(h * 128, 128)],
                raw.at[slot, pl.ds((h * 4 + f) * STRIP, STRIP)],
                in_sem.at[slot, h * 4 + f],
            )
            for h in range(2)
            for f in range(4)
        ]

    for c in load_fields(inflight_ref.at[0], 0):
        c.start()
    cls_copy = pltpu.make_async_copy(classes_ref.at[0], raw_cls, in_sem.at[TURNS, 0])
    cls_copy.start()

    @pl.when(d == 0)
    def _():
        for t in range(TURNS - 1):
            for c in load_fields(entering_ref.at[t], t + 1):
                c.start()

    bar = pltpu.get_barrier_semaphore()
    has_up, has_dn, has_next, has_prev = l > 0, l < L - 1, d < D - 1, d > 0

    def greet(cond, dd, dl):
        @pl.when(cond)
        def _():
            pl.semaphore_signal(bar, inc=1, device_id=(d + dd, l + dl), device_id_type=MESH)

    greet(has_up, 0, -1)
    greet(has_dn, 0, 1)
    greet(has_prev, -1, 0)
    greet(jnp.logical_and(has_prev, has_up), -1, -1)
    greet(jnp.logical_and(has_prev, has_dn), -1, 1)

    zero = jnp.zeros((8, 128), jnp.float32)

    @pl.when(l == 0)
    def _():
        cls_up[...] = jnp.zeros_like(cls_up)

    @pl.when(l == L - 1)
    def _():
        cls_dn[...] = jnp.zeros_like(cls_dn)

    def reflect(t):
        @pl.when(l == 0)
        def _():
            pr[t, HALO - 1] = zero
            for j in range(1, HALO):
                pr[t, HALO - 1 - j] = -pr[t, HALO - 1 + j]

        @pl.when(l == L - 1)
        def _():
            pr[t, HALO + STRIP] = zero
            for j in range(1, HALO):
                pr[t, HALO + STRIP + j] = -pr[t, HALO + STRIP - j]

    keep = jnp.where(
        low, jnp.where(l > 0, 1.0, 0.0).astype(jnp.float32), jnp.where(l < L - 1, 1.0, 0.0).astype(jnp.float32)
    )

    pack_idx = 2 * jnp.bitwise_and(lane, 63) + jnp.where(low, 0, 1)
    pack_direct = (lane < 64) == low

    def pack_fields(slot):
        def body(y, _):
            v = raw[slot, pl.ds(y, 8, stride=STRIP), :]
            a = lane_gather(v, pack_idx)
            b = lane_gather(roll4(v), pack_idx)
            pr[slot, HALO + y] = jnp.where(pack_direct, a, b)
            return 0

        lax.fori_loop(0, STRIP, body, 0, unroll=8)

    for c in load_fields(inflight_ref.at[0], 0):
        c.wait()
    pack_fields(0)

    n_lat = has_up.astype(jnp.int32) + has_dn.astype(jnp.int32)
    pl.semaphore_wait(bar, n_lat + has_next.astype(jnp.int32) * (1 + n_lat))
    cls_copy.wait()

    def to_up(src, slot, dd, sem):
        return pltpu.make_async_remote_copy(
            src, pr.at[slot, pl.ds(HALO + STRIP, HALO)], sem, rsem.at[slot, 1],
            device_id=(d + dd, l - 1), device_id_type=MESH,
        )

    def to_dn(src, slot, dd, sem):
        return pltpu.make_async_remote_copy(
            src, pr.at[slot, pl.ds(0, HALO)], sem, rsem.at[slot, 2],
            device_id=(d + dd, l + 1), device_id_type=MESH,
        )

    def lat_sends(slot):
        up = to_up(pr.at[slot, pl.ds(HALO, HALO)], slot, 0, esem.at[slot, 0])
        dn = to_dn(pr.at[slot, pl.ds(STRIP, HALO)], slot, 0, esem.at[slot, 1])
        return up, dn

    def cls_sends():
        up = pltpu.make_async_remote_copy(
            raw_cls.at[pl.ds(0, 8)], cls_dn, cssem.at[0], crsem.at[0], device_id=(d, l - 1), device_id_type=MESH
        )
        dn = pltpu.make_async_remote_copy(
            raw_cls.at[pl.ds(STRIP - 8, 8)], cls_up, cssem.at[1], crsem.at[1], device_id=(d, l + 1), device_id_type=MESH
        )
        return up, dn

    @pl.when(has_up)
    def _():
        lat_sends(0)[0].start()
        cls_sends()[0].start()

    @pl.when(has_dn)
    def _():
        lat_sends(0)[1].start()
        cls_sends()[1].start()

    @pl.when(d == 0)
    def _():
        for t in range(1, TURNS):
            for c in load_fields(entering_ref.at[t - 1], t):
                c.wait()
            pack_fields(t)

    @pl.when(jnp.logical_and(d == 0, has_up))
    def _():
        for t in range(1, TURNS):
            lat_sends(t)[0].start()

    @pl.when(jnp.logical_and(d == 0, has_dn))
    def _():
        for t in range(1, TURNS):
            lat_sends(t)[1].start()

    cid = jnp.bitwise_and(lane, 31)
    slow = jnp.zeros((8, 128), jnp.float32)
    for c in range(32):
        slow = jnp.where(cid == c, slow_ref[c], slow)
    for t in range(TURNS):
        inv = 1.0 / (freq_ref[t + D - 1 - d] * slow)
        values = [None] * (miller_start + 1)
        upper = jnp.zeros_like(inv)
        current = jnp.ones_like(inv)
        values[miller_start] = current
        for k in range(miller_start, 0, -1):
            lower = (2.0 * k * inv) * current - upper
            values[k - 1] = lower
            upper, current = current, lower
        evens = values[2]
        for k in range(4, miller_start + 1, 2):
            evens = evens + values[k]
        scale = 1.0 / (values[0] + 2.0 * evens)
        for k in range(TERMS):
            sign = -1.0 if (k // 2) % 2 else 1.0
            table[t, k] = values[k] * scale * (sign if k == 0 else 2.0 * sign)

    half_lane = lane < 64
    even_idx = 2 * jnp.bitwise_and(lane, 63)

    def fold_classes(i, top, top_row, bottom, bottom_row):
        sides = []
        for h in range(2):
            a = jnp.broadcast_to(top[pl.ds(top_row, 1), h * 128 : (h + 1) * 128], (8, 128))
            b = jnp.broadcast_to(bottom[pl.ds(bottom_row, 1), h * 128 : (h + 1) * 128], (8, 128))
            sides.append(jnp.where(low, a, b))
        for p in range(2):
            cls[i, p] = jnp.where(
                half_lane, lane_gather(sides[0], even_idx + p), lane_gather(sides[1], even_idx + p)
            )

    @pl.when(has_up)
    def _():
        cls_sends()[1].wait_recv()

    @pl.when(has_dn)
    def _():
        cls_sends()[0].wait_recv()

    for i in range(4):
        fold_classes(i, cls_up, 4 + i, cls_dn, 3 - i)
    for i in range(4, KEPT):
        fold_classes(i, raw_cls, i - 4, raw_cls, STRIP + 3 - i)

    def look_up(t):
        def body(i, _):
            for p in range(2):
                c = cls[i, p]
                for k in range(TERMS):
                    coef[k, i, p] = lane_gather(table[t, k], c)
            return 0

        lax.fori_loop(0, KEPT, body, 0)

    def step(cur, prev, low_row, top_row, k):
        first, even = k == 1, k % 2 == 0
        acc = acc_e if even else acc_o
        c1 = corner_weight * (1.0 if first else 2.0)
        c2 = delta * (1.0 if first else 2.0)
        above = [cur[low_row - 1, p] for p in range(2)]
        here = [cur[low_row, p] for p in range(2)]
        for i in range(low_row, top_row):
            if i < FOLD - 1:
                below = [cur[i + 1, p] for p in range(2)]
            else:
                below = [roll4(v) for v in here]
            w = [(above[p] + below[p]) + kappa * here[p] for p in range(2)]
            from_odd = jnp.where(lane == 0, 0.0, pltpu.roll(w[1], 1, 1))
            from_even = jnp.where(lane == 127, 0.0, pltpu.roll(w[0], 127, 1))
            x = [from_odd + w[1], w[0] + from_even]
            for p in range(2):
                f = c1 * (x[p] + kappa * w[p]) + c2 * here[p]
                if not first:
                    f = f - prev[i, p]
                prev[i, p] = f
                if i >= REACH:
                    j = i - REACH
                    if first:
                        acc[j, p] = coef[k, j, p] * f
                    else:
                        acc[j, p] = acc[j, p] + coef[k, j, p] * f
            above, here = here, below

    swap_sign = jnp.where(jnp.logical_or(jnp.bitwise_and(sub, 3) == 0, jnp.bitwise_and(sub, 3) == 3), -1.0, 1.0).astype(jnp.float32)
    even_sub = jnp.bitwise_and(sub, 1) == 0

    def extrapolate(t, halo_wait):
        def unfold(i):
            a = pr[t, i]
            b = pr[t, ROWS - 1 - i]
            return jnp.where(low, a, roll4(b)), jnp.where(low, roll4(a), b)

        def start(i):
            e, o = unfold(i)
            ta[i, 0] = e
            ta[i, 1] = o
            if i >= REACH:
                acc_e[i - REACH, 0] = coef[0, i - REACH, 0] * e
                acc_e[i - REACH, 1] = coef[0, i - REACH, 1] * o

        bufs = (ta, tb)
        halo_wait()
        reflect(t)
        for i in range(FOLD):
            start(i)
        for k in range(1, TERMS):
            step(bufs[(k - 1) % 2], bufs[k % 2], k, FOLD, k)

        def join(i, inside):
            out = []
            for p in range(2):
                o = acc_o[i, p]
                swapped = jnp.where(even_sub, pltpu.roll(o, 7, 0), pltpu.roll(o, 1, 0))
                value = acc_e[i, p] + swap_sign * swapped
                out.append(value if inside else value * keep)
            adv[t, i] = jnp.where(low, out[0], roll4(out[1]))
            adv[t, 2 * KEPT - 1 - i] = jnp.where(low, roll4(out[0]), out[1])

        for i in range(KEPT):
            join(i, i >= HALO - REACH)

    def correlate(t):
        def spread(r, _):
            std[pl.ds(r, 8, stride=PLANE), :] = adv[t, r]
            return 0

        lax.fori_loop(0, 2 * KEPT, spread, 0, unroll=8)
        for p in range(2):
            for b in range(STRIP // 8):
                for o in range(OFFSETS):
                    g = o - OFFSETS // 2
                    s0 = std[pl.ds((p * 4 + 0) * PLANE + 4 - g + 8 * b, 8), :]
                    s1 = std[pl.ds((p * 4 + 1) * PLANE + 4 - g + 8 * b, 8), :]
                    r0 = std[pl.ds((p * 4 + 2) * PLANE + 4 + g + 8 * b, 8), :]
                    r1 = std[pl.ds((p * 4 + 3) * PLANE + 4 + g + 8 * b, 8), :]
                    value = s0 * r0 + s1 * r1
                    if t > 0:
                        value = value + img[p, o, b]
                    img[p, o, b] = value

    def hand_over(t):
        n = t + 1
        strip = pltpu.make_async_remote_copy(
            adv.at[t, pl.ds(4, STRIP)], pr.at[n, pl.ds(HALO, STRIP)], ssem.at[t, 0], rsem.at[n, 0],
            device_id=(d + 1, l), device_id_type=MESH,
        )
        up = to_up(adv.at[t, pl.ds(4, HALO)], n, 1, ssem.at[t, 1])
        dn = to_dn(adv.at[t, pl.ds(4 + STRIP - HALO, HALO)], n, 1, ssem.at[t, 2])
        return strip, up, dn

    next_up = jnp.logical_and(has_next, has_up)
    next_dn = jnp.logical_and(has_next, has_dn)

    def for_each_send(t, act):
        for cond, which in ((next_up, 1), (next_dn, 2), (has_next, 0)):
            @pl.when(cond)
            def _():
                act(hand_over(t)[which])

    def wait_halo(t):
        @pl.when(has_dn)
        def _():
            lat_sends(t)[0].wait_recv()

        @pl.when(has_up)
        def _():
            lat_sends(t)[1].wait_recv()

    look_up(0)
    for t in range(TURNS):
        if t > 0:
            @pl.when(has_prev)
            def _():
                hand_over(t - 1)[0].wait_recv()
        extrapolate(t, lambda: wait_halo(t))
        if t + 1 < TURNS:
            for_each_send(t, lambda c: c.start())
            correlate(t)
            look_up(t + 1)

    join_idx = lax.shift_right_logical(lane, 1) + jnp.where(low, 0, 64)
    join_direct = (jnp.bitwise_and(lane, 1) == 0) == low

    def put(y, _):
        v = adv[TURNS - 1, 4 + y]
        a = lane_gather(v, join_idx)
        b = lane_gather(roll4(v), join_idx)
        wout[pl.ds(y, 8, stride=STRIP), :] = jnp.where(join_direct, a, b)
        return 0

    lax.fori_loop(0, STRIP, put, 0, unroll=8)

    def stores():
        return [
            pltpu.make_async_copy(
                wout.at[pl.ds((h * 4 + f) * STRIP, STRIP)],
                wave_ref.at[0, f, :, pl.ds(h * 128, 128)],
                out_sem.at[h * 4 + f],
            )
            for h in range(2)
            for f in range(4)
        ]

    for c in stores():
        c.start()
    correlate(TURNS - 1)
    half_idx = lax.shift_right_logical(lane, 1)
    even_lane = jnp.bitwise_and(lane, 1) == 0
    for o in range(OFFSETS):
        for b in range(STRIP // 8):
            e, q = img[0, o, b], img[1, o, b]
            for h in range(2):
                images_ref[0, o, pl.ds(8 * b, 8), pl.ds(128 * h, 128)] = jnp.where(
                    even_lane, lane_gather(e, half_idx + 64 * h), lane_gather(q, half_idx + 64 * h)
                )

    @pl.when(has_up)
    def _():
        lat_sends(0)[0].wait_send()
        cls_sends()[0].wait_send()

    @pl.when(has_dn)
    def _():
        lat_sends(0)[1].wait_send()
        cls_sends()[1].wait_send()

    @pl.when(jnp.logical_and(d == 0, has_up))
    def _():
        for t in range(1, TURNS):
            lat_sends(t)[0].wait_send()

    @pl.when(jnp.logical_and(d == 0, has_dn))
    def _():
        for t in range(1, TURNS):
            lat_sends(t)[1].wait_send()

    for t in range(TURNS - 1):
        for_each_send(t, lambda c: c.wait_send())
    for c in stores():
        c.wait()


def local(in_flight, entering, classes, freq_phase, class_slowness):
    any_space = pl.BlockSpec(memory_space=pl.ANY)
    smem = pl.BlockSpec(memory_space=pltpu.SMEM)
    f32, i32 = jnp.float32, jnp.int32
    dma = pltpu.SemaphoreType.DMA
    return pl.pallas_call(
        kernel,
        out_shape=(
            pltpu.VMEM((1, OFFSETS, STRIP, 256), f32),
            pltpu.VMEM((1, 4, STRIP, 256), f32),
        ),
        in_specs=[any_space, any_space, any_space, smem, smem],
        out_specs=(pl.BlockSpec(memory_space=pltpu.VMEM), pl.BlockSpec(memory_space=pltpu.VMEM)),
        scratch_shapes=[
            pltpu.VMEM((TURNS, 8 * STRIP, 128), f32),
            pltpu.VMEM((STRIP, 256), i32),
            pltpu.VMEM((8, 256), i32),
            pltpu.VMEM((8, 256), i32),
            pltpu.VMEM((TURNS, ROWS, 8, 128), f32),
            pltpu.VMEM((TURNS, 2 * KEPT, 8, 128), f32),
            pltpu.VMEM((FOLD, 2, 8, 128), f32),
            pltpu.VMEM((FOLD, 2, 8, 128), f32),
            pltpu.VMEM((KEPT, 2, 8, 128), f32),
            pltpu.VMEM((KEPT, 2, 8, 128), f32),
            pltpu.VMEM((TERMS, KEPT, 2, 8, 128), f32),
            pltpu.VMEM((KEPT, 2, 8, 128), i32),
            pltpu.VMEM((TURNS, TERMS, 8, 128), f32),
            pltpu.VMEM((8 * PLANE, 128), f32),
            pltpu.VMEM((2, OFFSETS, STRIP // 8, 8, 128), f32),
            pltpu.VMEM((8 * STRIP, 128), f32),
            dma((TURNS + 1, 8)),
            dma((8,)),
            dma((TURNS - 1, 3)),
            dma((TURNS, 3)),
            dma((TURNS, 2)),
            dma((2,)),
            dma((2,)),
        ],
        compiler_params=pltpu.CompilerParams(
            collective_id=0, has_side_effects=True, vmem_limit_bytes=56 * 2**20
        ),
        cost_estimate=pl.CostEstimate(flops=60_000_000, bytes_accessed=1_000_000, transcendentals=0),
    )(in_flight, entering, classes, freq_phase, class_slowness)


def solution(mesh):
    in_specs = (
        P("depth", None, "lat", None),
        P(None, None, "lat", None),
        P("depth", "lat", None),
        P(),
        P(),
    )
    out_specs = (P("depth", None, "lat", None), P("depth", None, "lat", None))
    return jax.shard_map(local, mesh=mesh, in_specs=in_specs, out_specs=out_specs, check_vma=False)
```

```python
import jax
import jax.numpy as jnp
from jax import lax
from jax.experimental import pallas as pl
from jax.experimental.pallas import tpu as pltpu
from jax.sharding import PartitionSpec as P

TERMS = 16
OFFSETS = 8
TURNS = 3
STRIP = 32
HALO = 19
ROWS = STRIP + 2 * HALO
FOLD = ROWS // 2
REACH = 15
KEPT = FOLD - REACH
PLANE = 48
MESH = pl.DeviceIdType.MESH

hale_weight = 0.0255
centre_weight = -0.5 + hale_weight
edge_weight = 0.25 - 0.5 * hale_weight
corner_weight = 0.125 + 0.25 * hale_weight
kappa = edge_weight / corner_weight
delta = centre_weight - edge_weight * kappa
miller_start = 32


def lane_gather(x, idx):
    numbers = lax.GatherDimensionNumbers(
        offset_dims=(),
        collapsed_slice_dims=(1,),
        start_index_map=(1,),
        operand_batching_dims=(0,),
        start_indices_batching_dims=(0,),
    )
    return lax.gather(
        x, idx[:, :, None], numbers, (1, 1), mode=lax.GatherScatterMode.PROMISE_IN_BOUNDS
    )


def kernel(
    inflight_ref, entering_ref, classes_ref, freq_ref, slow_ref,
    images_ref, wave_ref,
    raw, raw_cls, cls_up, cls_dn, pr, adv, ta, tb, acc_e, acc_o, coef, cls, table, std,
    in_sem, ssem, rsem, esem, cssem, crsem,
):
    d = lax.axis_index("depth")
    l = lax.axis_index("lat")
    D = lax.axis_size("depth")
    L = lax.axis_size("lat")

    sub = lax.broadcasted_iota(jnp.int32, (8, 128), 0)
    lane = lax.broadcasted_iota(jnp.int32, (8, 128), 1)
    low = sub < 4

    def roll4(x):
        return pltpu.roll(x, 4, 0)

    def load_fields(src, slot):
        return [
            pltpu.make_async_copy(
                src.at[f, :, pl.ds(h * 128, 128)],
                raw.at[slot, pl.ds((h * 4 + f) * STRIP, STRIP)],
                in_sem.at[slot, h * 4 + f],
            )
            for h in range(2)
            for f in range(4)
        ]

    for c in load_fields(inflight_ref.at[0], 0):
        c.start()
    cls_copy = pltpu.make_async_copy(classes_ref.at[0], raw_cls, in_sem.at[TURNS, 0])
    cls_copy.start()

    @pl.when(d == 0)
    def _():
        for t in range(TURNS - 1):
            for c in load_fields(entering_ref.at[t], t + 1):
                c.start()

    bar = pltpu.get_barrier_semaphore()
    has_up, has_dn, has_next, has_prev = l > 0, l < L - 1, d < D - 1, d > 0

    def greet(cond, dd, dl):
        @pl.when(cond)
        def _():
            pl.semaphore_signal(bar, inc=1, device_id=(d + dd, l + dl), device_id_type=MESH)

    greet(has_up, 0, -1)
    greet(has_dn, 0, 1)
    greet(has_prev, -1, 0)
    greet(jnp.logical_and(has_prev, has_up), -1, -1)
    greet(jnp.logical_and(has_prev, has_dn), -1, 1)

    zero = jnp.zeros((8, 128), jnp.float32)

    @pl.when(l == 0)
    def _():
        cls_up[...] = jnp.zeros_like(cls_up)

    @pl.when(l == L - 1)
    def _():
        cls_dn[...] = jnp.zeros_like(cls_dn)

    def reflect(t):
        @pl.when(l == 0)
        def _():
            pr[t, HALO - 1] = zero
            for j in range(1, HALO):
                pr[t, HALO - 1 - j] = -pr[t, HALO - 1 + j]

        @pl.when(l == L - 1)
        def _():
            pr[t, HALO + STRIP] = zero
            for j in range(1, HALO):
                pr[t, HALO + STRIP + j] = -pr[t, HALO + STRIP - j]

    keep = jnp.where(
        low, jnp.where(l > 0, 1.0, 0.0).astype(jnp.float32), jnp.where(l < L - 1, 1.0, 0.0).astype(jnp.float32)
    )

    pack_idx = 2 * jnp.bitwise_and(lane, 63) + jnp.where(low, 0, 1)
    pack_direct = (lane < 64) == low

    def pack_fields(slot):
        def body(y, _):
            v = raw[slot, pl.ds(y, 8, stride=STRIP), :]
            a = lane_gather(v, pack_idx)
            b = lane_gather(roll4(v), pack_idx)
            pr[slot, HALO + y] = jnp.where(pack_direct, a, b)
            return 0

        lax.fori_loop(0, STRIP, body, 0, unroll=8)

    for c in load_fields(inflight_ref.at[0], 0):
        c.wait()
    pack_fields(0)

    n_lat = has_up.astype(jnp.int32) + has_dn.astype(jnp.int32)
    pl.semaphore_wait(bar, n_lat + has_next.astype(jnp.int32) * (1 + n_lat))
    cls_copy.wait()

    def to_up(src, slot, dd, sem):
        return pltpu.make_async_remote_copy(
            src, pr.at[slot, pl.ds(HALO + STRIP, HALO)], sem, rsem.at[slot, 1],
            device_id=(d + dd, l - 1), device_id_type=MESH,
        )

    def to_dn(src, slot, dd, sem):
        return pltpu.make_async_remote_copy(
            src, pr.at[slot, pl.ds(0, HALO)], sem, rsem.at[slot, 2],
            device_id=(d + dd, l + 1), device_id_type=MESH,
        )

    def lat_sends(slot):
        up = to_up(pr.at[slot, pl.ds(HALO, HALO)], slot, 0, esem.at[slot, 0])
        dn = to_dn(pr.at[slot, pl.ds(STRIP, HALO)], slot, 0, esem.at[slot, 1])
        return up, dn

    def cls_sends():
        up = pltpu.make_async_remote_copy(
            raw_cls.at[pl.ds(0, 8)], cls_dn, cssem.at[0], crsem.at[0], device_id=(d, l - 1), device_id_type=MESH
        )
        dn = pltpu.make_async_remote_copy(
            raw_cls.at[pl.ds(STRIP - 8, 8)], cls_up, cssem.at[1], crsem.at[1], device_id=(d, l + 1), device_id_type=MESH
        )
        return up, dn

    @pl.when(has_up)
    def _():
        lat_sends(0)[0].start()
        cls_sends()[0].start()

    @pl.when(has_dn)
    def _():
        lat_sends(0)[1].start()
        cls_sends()[1].start()

    @pl.when(d == 0)
    def _():
        for t in range(1, TURNS):
            for c in load_fields(entering_ref.at[t - 1], t):
                c.wait()
            pack_fields(t)

    @pl.when(jnp.logical_and(d == 0, has_up))
    def _():
        for t in range(1, TURNS):
            lat_sends(t)[0].start()

    @pl.when(jnp.logical_and(d == 0, has_dn))
    def _():
        for t in range(1, TURNS):
            lat_sends(t)[1].start()

    cid = jnp.bitwise_and(lane, 31)
    slow = jnp.zeros((8, 128), jnp.float32)
    for c in range(32):
        slow = jnp.where(cid == c, slow_ref[c], slow)
    for t in range(TURNS):
        inv = 1.0 / (freq_ref[t + D - 1 - d] * slow)
        values = [None] * (miller_start + 1)
        upper = jnp.zeros_like(inv)
        current = jnp.ones_like(inv)
        values[miller_start] = current
        for k in range(miller_start, 0, -1):
            lower = (2.0 * k * inv) * current - upper
            values[k - 1] = lower
            upper, current = current, lower
        evens = values[2]
        for k in range(4, miller_start + 1, 2):
            evens = evens + values[k]
        scale = 1.0 / (values[0] + 2.0 * evens)
        for k in range(TERMS):
            sign = -1.0 if (k // 2) % 2 else 1.0
            table[t, k] = values[k] * scale * (sign if k == 0 else 2.0 * sign)

    half_lane = lane < 64
    even_idx = 2 * jnp.bitwise_and(lane, 63)

    def fold_classes(i, top, top_row, bottom, bottom_row):
        sides = []
        for h in range(2):
            a = jnp.broadcast_to(top[pl.ds(top_row, 1), h * 128 : (h + 1) * 128], (8, 128))
            b = jnp.broadcast_to(bottom[pl.ds(bottom_row, 1), h * 128 : (h + 1) * 128], (8, 128))
            sides.append(jnp.where(low, a, b))
        for p in range(2):
            cls[i, p] = jnp.where(
                half_lane, lane_gather(sides[0], even_idx + p), lane_gather(sides[1], even_idx + p)
            )

    @pl.when(has_up)
    def _():
        cls_sends()[1].wait_recv()

    @pl.when(has_dn)
    def _():
        cls_sends()[0].wait_recv()

    for i in range(4):
        fold_classes(i, cls_up, 4 + i, cls_dn, 3 - i)
    for i in range(4, KEPT):
        fold_classes(i, raw_cls, i - 4, raw_cls, STRIP + 3 - i)

    def look_up(t):
        def body(i, _):
            for p in range(2):
                c = cls[i, p]
                for k in range(TERMS):
                    coef[k, i, p] = lane_gather(table[t, k], c)
            return 0

        lax.fori_loop(0, KEPT, body, 0)

    def step(cur, prev, low_row, top_row, k):
        first, even = k == 1, k % 2 == 0
        acc = acc_e if even else acc_o
        c1 = corner_weight * (1.0 if first else 2.0)
        c2 = delta * (1.0 if first else 2.0)
        above = [cur[low_row - 1, p] for p in range(2)]
        here = [cur[low_row, p] for p in range(2)]
        for i in range(low_row, top_row):
            if i < FOLD - 1:
                below = [cur[i + 1, p] for p in range(2)]
            else:
                below = [roll4(v) for v in here]
            w = [(above[p] + below[p]) + kappa * here[p] for p in range(2)]
            from_odd = jnp.where(lane == 0, 0.0, pltpu.roll(w[1], 1, 1))
            from_even = jnp.where(lane == 127, 0.0, pltpu.roll(w[0], 127, 1))
            x = [from_odd + w[1], w[0] + from_even]
            for p in range(2):
                f = c1 * (x[p] + kappa * w[p]) + c2 * here[p]
                if not first:
                    f = f - prev[i, p]
                prev[i, p] = f
                if i >= REACH:
                    j = i - REACH
                    if first:
                        acc[j, p] = coef[k, j, p] * f
                    else:
                        acc[j, p] = acc[j, p] + coef[k, j, p] * f
            above, here = here, below

    swap_sign = jnp.where(jnp.logical_or(jnp.bitwise_and(sub, 3) == 0, jnp.bitwise_and(sub, 3) == 3), -1.0, 1.0).astype(jnp.float32)
    even_sub = jnp.bitwise_and(sub, 1) == 0

    def extrapolate(t, halo_wait):
        def unfold(i):
            a = pr[t, i]
            b = pr[t, ROWS - 1 - i]
            return jnp.where(low, a, roll4(b)), jnp.where(low, roll4(a), b)

        def start(i):
            e, o = unfold(i)
            ta[i, 0] = e
            ta[i, 1] = o
            if i >= REACH:
                acc_e[i - REACH, 0] = coef[0, i - REACH, 0] * e
                acc_e[i - REACH, 1] = coef[0, i - REACH, 1] * o

        bufs = (ta, tb)
        halo_wait()
        reflect(t)
        for i in range(FOLD):
            start(i)
        for k in range(1, TERMS):
            step(bufs[(k - 1) % 2], bufs[k % 2], k, FOLD, k)

        def join(i, inside):
            out = []
            for p in range(2):
                o = acc_o[i, p]
                swapped = jnp.where(even_sub, pltpu.roll(o, 7, 0), pltpu.roll(o, 1, 0))
                value = acc_e[i, p] + swap_sign * swapped
                out.append(value if inside else value * keep)
            adv[t, i] = jnp.where(low, out[0], roll4(out[1]))
            adv[t, 2 * KEPT - 1 - i] = jnp.where(low, roll4(out[0]), out[1])

        for i in range(KEPT):
            join(i, i >= HALO - REACH)

    join_idx = lax.shift_right_logical(lane, 1) + jnp.where(low, 0, 64)
    join_direct = (jnp.bitwise_and(lane, 1) == 0) == low

    def correlate(t):
        def spread(r, _):
            v = adv[t, r]
            natural = jnp.where(join_direct, lane_gather(v, join_idx), lane_gather(roll4(v), join_idx))
            std[pl.ds(r, 8, stride=PLANE), :] = natural
            return 0

        lax.fori_loop(0, 2 * KEPT, spread, 0, unroll=8)
        for h in range(2):
            for b in range(STRIP // 8):
                rows, columns = pl.ds(8 * b, 8), pl.ds(128 * h, 128)
                if t == TURNS - 1:
                    for f in range(4):
                        wave_ref[0, f, rows, columns] = std[pl.ds((h * 4 + f) * PLANE + 4 + 8 * b, 8), :]
                for o in range(OFFSETS):
                    g = o - OFFSETS // 2
                    s0 = std[pl.ds((h * 4 + 0) * PLANE + 4 - g + 8 * b, 8), :]
                    s1 = std[pl.ds((h * 4 + 1) * PLANE + 4 - g + 8 * b, 8), :]
                    r0 = std[pl.ds((h * 4 + 2) * PLANE + 4 + g + 8 * b, 8), :]
                    r1 = std[pl.ds((h * 4 + 3) * PLANE + 4 + g + 8 * b, 8), :]
                    value = s0 * r0 + s1 * r1
                    if t > 0:
                        value = value + images_ref[0, o, rows, columns]
                    images_ref[0, o, rows, columns] = value

    def hand_over(t):
        n = t + 1
        strip = pltpu.make_async_remote_copy(
            adv.at[t, pl.ds(4, STRIP)], pr.at[n, pl.ds(HALO, STRIP)], ssem.at[t, 0], rsem.at[n, 0],
            device_id=(d + 1, l), device_id_type=MESH,
        )
        up = to_up(adv.at[t, pl.ds(4, HALO)], n, 1, ssem.at[t, 1])
        dn = to_dn(adv.at[t, pl.ds(4 + STRIP - HALO, HALO)], n, 1, ssem.at[t, 2])
        return strip, up, dn

    next_up = jnp.logical_and(has_next, has_up)
    next_dn = jnp.logical_and(has_next, has_dn)

    def for_each_send(t, act):
        for cond, which in ((next_up, 1), (next_dn, 2), (has_next, 0)):
            @pl.when(cond)
            def _():
                act(hand_over(t)[which])

    def wait_halo(t):
        @pl.when(has_dn)
        def _():
            lat_sends(t)[0].wait_recv()

        @pl.when(has_up)
        def _():
            lat_sends(t)[1].wait_recv()

    look_up(0)
    for t in range(TURNS):
        if t > 0:
            @pl.when(has_prev)
            def _():
                hand_over(t - 1)[0].wait_recv()
        extrapolate(t, lambda: wait_halo(t))
        if t + 1 < TURNS:
            for_each_send(t, lambda c: c.start())
            correlate(t)
            look_up(t + 1)

    correlate(TURNS - 1)

    @pl.when(has_up)
    def _():
        lat_sends(0)[0].wait_send()
        cls_sends()[0].wait_send()

    @pl.when(has_dn)
    def _():
        lat_sends(0)[1].wait_send()
        cls_sends()[1].wait_send()

    @pl.when(jnp.logical_and(d == 0, has_up))
    def _():
        for t in range(1, TURNS):
            lat_sends(t)[0].wait_send()

    @pl.when(jnp.logical_and(d == 0, has_dn))
    def _():
        for t in range(1, TURNS):
            lat_sends(t)[1].wait_send()

    for t in range(TURNS - 1):
        for_each_send(t, lambda c: c.wait_send())


def local(in_flight, entering, classes, freq_phase, class_slowness):
    any_space = pl.BlockSpec(memory_space=pl.ANY)
    smem = pl.BlockSpec(memory_space=pltpu.SMEM)
    f32, i32 = jnp.float32, jnp.int32
    dma = pltpu.SemaphoreType.DMA
    return pl.pallas_call(
        kernel,
        out_shape=(
            pltpu.VMEM((1, OFFSETS, STRIP, 256), f32),
            pltpu.VMEM((1, 4, STRIP, 256), f32),
        ),
        in_specs=[any_space, any_space, any_space, smem, smem],
        out_specs=(pl.BlockSpec(memory_space=pltpu.VMEM), pl.BlockSpec(memory_space=pltpu.VMEM)),
        scratch_shapes=[
            pltpu.VMEM((TURNS, 8 * STRIP, 128), f32),
            pltpu.VMEM((STRIP, 256), i32),
            pltpu.VMEM((8, 256), i32),
            pltpu.VMEM((8, 256), i32),
            pltpu.VMEM((TURNS, ROWS, 8, 128), f32),
            pltpu.VMEM((TURNS, 2 * KEPT, 8, 128), f32),
            pltpu.VMEM((FOLD, 2, 8, 128), f32),
            pltpu.VMEM((FOLD, 2, 8, 128), f32),
            pltpu.VMEM((KEPT, 2, 8, 128), f32),
            pltpu.VMEM((KEPT, 2, 8, 128), f32),
            pltpu.VMEM((TERMS, KEPT, 2, 8, 128), f32),
            pltpu.VMEM((KEPT, 2, 8, 128), i32),
            pltpu.VMEM((TURNS, TERMS, 8, 128), f32),
            pltpu.VMEM((8 * PLANE, 128), f32),
            dma((TURNS + 1, 8)),
            dma((TURNS - 1, 3)),
            dma((TURNS, 3)),
            dma((TURNS, 2)),
            dma((2,)),
            dma((2,)),
        ],
        compiler_params=pltpu.CompilerParams(
            collective_id=0, has_side_effects=True, vmem_limit_bytes=56 * 2**20
        ),
        cost_estimate=pl.CostEstimate(flops=60_000_000, bytes_accessed=1_000_000, transcendentals=0),
    )(in_flight, entering, classes, freq_phase, class_slowness)


def solution(mesh):
    in_specs = (
        P("depth", None, "lat", None),
        P(None, None, "lat", None),
        P("depth", "lat", None),
        P(),
        P(),
    )
    out_specs = (P("depth", None, "lat", None), P("depth", None, "lat", None))
    return jax.shard_map(local, mesh=mesh, in_specs=in_specs, out_specs=out_specs, check_vma=False)
```
